32 devices in a mesh: prow: 4 (over y, core), pcol: 8 (over z, x).
Axes of the slice: x: 2, y: 2, z: 4, core: 2. Of those that a mesh axis runs over, the one named last changes fastest.
Arguments:
- parent: float32 [12, 4, 256, 6, 8, 256], P(None, 'prow', None, None, 'pcol')
- children: float32 [8, 4, 256, 2, 8, 256], P(None, 'prow', None, None, 'pcol')
- index_maps: int32 [2, 16], replicated, may hold values from 0 to 47, as said below
Outputs:
- factored: float32 [12, 4, 256, 6, 8, 256], P(None, 'prow', None, None, 'pcol')
The draws below stay inside these ranges and needn't reach their ends.
Inputs may be any that keep to these rules, and one draw needn't show every extreme that they name: `index_maps`: entry (k, u) is 3 u, 3 u + 1 or 3 u + 2, so each row rises strictly. Of the blocks u of one child with one remainder modulo 2, at most 4 go to parent blocks of one remainder modulo 2 * 2.
All inputs are finite; a program needn't handle non-finite values.
Results may differ from the reference program's by a relative error of at most 0.00005.
Values sent between devices are 32-bit elements; how exact they have to be, the bound alone decides.
A program may use at most 192 MiB of HBM per device.

```python
import math
import jax
import jax.numpy as jnp
from jax import lax

NB = 256
PB = 48
UB = 16
KB = 5
HALF = 2
LR = 12
LC = 6
ULR = 8
ULC = 2
N_PROW = 4
N_PCOL = 8


parent_spread = 0.25


child_spread = 0.125


def symmetrize(raw_values, spread):
    return (raw_values + jnp.swapaxes(raw_values, -1, -2)) * (spread / math.sqrt(2.0))


def edge_bound():
    lead_blocks = (KB + 2) // 3
    return 2.0 * parent_spread * math.sqrt(KB * NB) + 4.0 * child_spread * math.sqrt(lead_blocks * NB)


def draw_parent(key, part):
    key = jax.random.fold_in(key, 11)
    first_key, second_key = jax.random.split(key)
    full_order = PB * NB
    bound_value = edge_bound()
    raw_values = jax.random.normal(first_key, (full_order, full_order), jnp.float32)
    diagonal = jax.random.uniform(second_key, (full_order,), jnp.float32, bound_value, 2.0 * bound_value)
    entries = symmetrize(raw_values, parent_spread)
    positions = jnp.arange(full_order)
    entries = entries.at[positions, positions].set(diagonal.astype(jnp.float32))
    return entries.reshape(LR, 2 * HALF, NB, LC, UB // ULC, NB).astype(jnp.float32)


def draw_children(key, part):
    key = jax.random.fold_in(key, 12)
    raw_values = jax.random.normal(key, (2, UB * NB, UB * NB), jnp.float32)
    entries = symmetrize(raw_values, child_spread)
    entries = entries.reshape(2, ULR, HALF, NB, ULC, UB // ULC, NB).transpose(1, 0, 2, 3, 4, 5, 6)
    return entries.reshape(ULR, 2 * HALF, NB, ULC, UB // ULC, NB).astype(jnp.float32)


def draw_index_maps(key, part):
    key = jax.random.fold_in(key, 13)
    first_key, second_key = jax.random.split(key)
    classes = 2 * HALF
    starts = jax.random.randint(first_key, (2, classes), 0, 3, jnp.int32)
    strides = jax.random.randint(second_key, (2, classes), 1, 3, jnp.int32)
    blocks = jnp.arange(UB, dtype=jnp.int32)
    last_class = (UB - 1) % classes
    last_turn = (UB - 1) // classes
    starts = starts.at[0, 0].set(0)
    starts = starts.at[1, last_class].set((2 - strides[1, last_class] * last_turn) % 3)
    turn_of = blocks // classes
    class_of = blocks % classes
    offsets = (starts[:, class_of] + strides[:, class_of] * turn_of[None, :]) % 3
    return (3 * blocks[None, :] + offsets).astype(jnp.int32)


def setup_inputs(seed: int = 0) -> dict:
    key_of = jax.random.split(jax.random.key(seed), 4)
    parent = draw_parent(jax.random.fold_in(key_of[3], 71), 0)
    children = draw_children(jax.random.fold_in(key_of[3], 71), 0)
    index_maps = draw_index_maps(jax.random.fold_in(key_of[3], 71), 0)
    return dict(parent=parent, children=children, index_maps=index_maps)


def reference(parent, children, index_maps):
    full_order = PB * NB
    front_full = parent.reshape(full_order, full_order)
    child_full = children.reshape(ULR, 2, HALF, NB, ULC, N_PCOL, NB)
    child_full = child_full.transpose(1, 0, 2, 3, 4, 5, 6).reshape(2, UB * NB, UB * NB)
    for child_index in range(2):
        positions = (index_maps[child_index][:, None] * NB + jnp.arange(NB, dtype=jnp.int32)[None, :]).reshape(-1).astype(jnp.int32)
        front_full = front_full.at[positions[:, None], positions[None, :]].add(child_full[child_index])
    panel_width = KB * NB
    leading = jnp.tril(jnp.linalg.cholesky(front_full[:panel_width, :panel_width]))
    lower_part = lax.linalg.triangular_solve(leading, front_full[panel_width:, :panel_width], left_side=False, lower=True, transpose_a=True)
    schur_part = front_full[panel_width:, panel_width:] - jnp.dot(lower_part.astype(jnp.float32), lower_part.T.astype(jnp.float32), precision=lax.Precision.HIGHEST, preferred_element_type=jnp.float32)
    upper_rows = jnp.concatenate([leading, jnp.zeros((panel_width, full_order - panel_width), jnp.float32)], axis=1)
    bottom_rows = jnp.concatenate([lower_part, schur_part], axis=1)
    result = jnp.concatenate([upper_rows, bottom_rows], axis=0)
    return result.reshape(LR, N_PROW, NB, LC, N_PCOL, NB)
```

```python
import functools
import jax
import jax.numpy as jnp

from jax import lax
from jax.sharding import PartitionSpec as P
from jax.experimental import pallas as pl
from jax.experimental.pallas import tpu as pltpu

KB = 5
SUB = 64


def mm(a, b):
    return lax.dot_general(a, b, (((1,), (0,)), ((), ())),
        precision=lax.Precision.HIGHEST, preferred_element_type=jnp.float32)


def mm_t(a, b):
    return lax.dot_general(a, b, (((1,), (1,)), ((), ())),
        precision=lax.Precision.HIGHEST, preferred_element_type=jnp.float32)


def small_factor(block):
    n = block.shape[0]
    rows = lax.broadcasted_iota(jnp.int32, (n, 1), 0)
    lanes = lax.broadcasted_iota(jnp.int32, (n, 2 * n), 1)
    rows2 = lax.broadcasted_iota(jnp.int32, (n, 2 * n), 0)
    eye = jnp.where(lanes - n == rows2, 1.0, 0.0).astype(jnp.float32)
    aug = jnp.concatenate([block, jnp.zeros_like(block)], axis=1) + eye
    for j in range(n):
        row = aug[j : j + 1, :]
        col = aug[:, j : j + 1]
        scaled = row * (1.0 / row[:, j : j + 1])
        aug = aug - jnp.where(rows > j, col, 0.0) * scaled
    square = jnp.where(lanes == rows2, aug, 0.0)
    pivot = jnp.sum(square, axis=1, keepdims=True)
    aug = aug * (1.0 / jnp.sqrt(pivot))
    upper = jnp.where(lanes[:, :n] >= rows2[:, :n], aug[:, :n], 0.0)
    return upper.T, aug[:, n:]


def factor_kernel(a_ref, l_ref, w_ref, d_ref):
    count, size = a_ref.shape[0], a_ref.shape[2]
    parts = size // SUB
    l_ref[...] = a_ref[...]

    @pl.loop(0, count)
    def _(k):
        d_ref[...] = l_ref[k, k]
        w_ref[k] = jnp.zeros((size, size), jnp.float32)
        for t in range(parts):
            lo, hi = t * SUB, (t + 1) * SUB
            low, inv = small_factor(d_ref[lo:hi, lo:hi])
            d_ref[lo:hi, lo:hi] = low
            if t + 1 < parts:
                d_ref[lo:hi, hi:size] = jnp.zeros((SUB, size - hi), jnp.float32)
                below = mm_t(d_ref[hi:size, lo:hi], inv)
                d_ref[hi:size, lo:hi] = below
                d_ref[hi:size, hi:size] = d_ref[hi:size, hi:size] - mm_t(below, below)
            w_ref[k, lo:hi, lo:hi] = inv
            if t:
                w_ref[k, lo:hi, 0:lo] = -mm(inv, mm(d_ref[lo:hi, 0:lo], w_ref[k, 0:lo, 0:lo]))
        l_ref[k, k] = d_ref[...]

        @pl.loop(k + 1, count)
        def _(i):
            l_ref[i, k] = mm_t(l_ref[i, k], w_ref[k])

        @pl.loop(k + 1, count)
        def _(i):
            @pl.loop(k + 1, i + 1)
            def _(j):
                l_ref[i, j] = l_ref[i, j] - mm_t(l_ref[i, k], l_ref[j, k])


def factor(a):
    count, size = a.shape[0], a.shape[2]
    return pl.pallas_call(
        factor_kernel,
        out_shape=(jax.ShapeDtypeStruct(a.shape, jnp.float32),
                   jax.ShapeDtypeStruct((count, size, size), jnp.float32)),
        in_specs=[pl.BlockSpec(memory_space=pltpu.VMEM)],
        out_specs=(pl.BlockSpec(memory_space=pltpu.VMEM),) * 2,
        scratch_shapes=[pltpu.VMEM((size, size), jnp.float32)],
        compiler_params=pltpu.CompilerParams(vmem_limit_bytes=40 << 20),
    )(a)


def place_kernel(row_ref, hit_ref, sec_ref, slot_ref, front_ref, first_ref, second_ref, out_ref):
    r, c = pl.program_id(0), pl.program_id(1)
    cols = pl.num_programs(1)
    total = front_ref[0]
    zero = jnp.zeros_like(total)
    total = total + jnp.where(hit_ref[0, r * cols + c] > 0, first_ref[0, 0], zero)
    total = total + jnp.where(hit_ref[1, r * cols + c] > 0, second_ref[0, 0], zero)
    out_ref[0] = total


def place(front, received, source, hit, section, slot):
    rows, size, width = front.shape
    cols = width // size

    def child_map(k):
        return lambda r, c, s, h, x, y: (s[k, r * cols + c], x[k, r * cols + c], 0, y[k, r * cols + c])

    return pl.pallas_call(
        place_kernel,
        grid_spec=pltpu.PrefetchScalarGridSpec(
            num_scalar_prefetch=4,
            grid=(rows, cols),
            in_specs=[
                pl.BlockSpec((1, size, size), lambda r, c, s, h, x, y: (r, 0, c)),
                pl.BlockSpec((1, 1, size, size), child_map(0)),
                pl.BlockSpec((1, 1, size, size), child_map(1)),
            ],
            out_specs=pl.BlockSpec((1, size, size), lambda r, c, s, h, x, y: (r, 0, c)),
        ),
        out_shape=jax.ShapeDtypeStruct(front.shape, front.dtype),
    )(source, hit, section, slot, front, received, received)


def per_device(parent, children, index_maps):
    prow_count = lax.axis_size("prow")
    pcol_count = lax.axis_size("pcol")
    prow_id = lax.axis_index("prow")
    pcol_id = lax.axis_index("pcol")
    half = prow_count // 2
    size = parent.shape[2]
    rows, cols = parent.shape[0], parent.shape[3]
    child_rows, child_cols = children.shape[0], children.shape[3]
    child_blocks = index_maps.shape[1]
    high = lax.Precision.HIGH
    front = parent.reshape(rows, size, cols * size)
    child = children.reshape(child_rows, size, child_cols * size)

    blocks = jnp.arange(child_blocks)
    dest = index_maps % prow_count
    earlier = (blocks[:, None] > blocks[None, :]) & (blocks[:, None] % half == blocks[None, :] % half)
    position = jnp.sum(earlier[None] & (dest[:, :, None] == dest[:, None, :]), axis=2)
    most = (child_rows // 2 + 2) // 3 * (2 - min(1, half // 3))

    sections = [
        lax.ppermute(child, "pcol", [(q, (3 * q + d) % pcol_count) for q in range(pcol_count)])
        for d in range(3)
    ]
    mine = (blocks // half)[None, :] * 0 + blocks[None, :] % half
    here = (jnp.arange(2)[:, None] == prow_id // half) & (mine == prow_id % half)
    wanted = (
        here[None, None]
        & (dest[None, None] == jnp.arange(prow_count)[:, None, None, None])
        & (position[None, None] == jnp.arange(most)[None, :, None, None])
    )
    index = jnp.sum(jnp.where(wanted, (blocks // half)[None, None, None, :], 0), axis=(2, 3))
    index = index.reshape(-1)
    received = []
    for section in sections:
        packed = jnp.take(section, index, axis=0).reshape(prow_count, most, size, child_cols * size)
        got = lax.all_to_all(packed, "prow", split_axis=0, concat_axis=0, tiled=True)
        received.append(got.reshape(prow_count * most, size, child_cols * size))
    received = jnp.stack(received, axis=1)

    row_ids = jnp.arange(rows) * prow_count + prow_id
    col_ids = jnp.arange(cols) * pcol_count + pcol_id

    def lookup(table, at):
        return jnp.sum(jnp.where(at[None, :, None] == blocks[None, None, :], table[:, None, :], 0), axis=2)

    u, v = row_ids // 3, col_ids // 3
    hit = (lookup(index_maps, u) == row_ids[None])[:, :, None] & (lookup(index_maps, v) == col_ids[None])[:, None, :]
    holder = jnp.arange(2)[:, None] * half + (u % half)[None, :]
    source = (holder * most + lookup(position, u))[:, :, None]
    shape = (2, rows, cols)
    source = jnp.where(hit, source, 0)
    section_id = jnp.where(hit, (col_ids % 3)[None, None, :], 0)
    slot = jnp.where(hit, (v // pcol_count)[None, None, :], 0)
    flat = lambda x: jnp.broadcast_to(x, shape).reshape(2, rows * cols).astype(jnp.int32)
    front = place(front, received, flat(source), flat(hit), flat(section_id), flat(slot))

    lead = -(-KB // prow_count)
    tops = lax.all_gather(front[:lead], "prow", axis=1, tiled=False)
    tops = tops.reshape(lead * prow_count, size, cols * size)[:KB]
    lefts = lax.all_gather(front[:, :, :size], "pcol", axis=0, tiled=False)[:KB]
    corner = lax.all_gather(tops[:, :, :size], "pcol", axis=1, tiled=False)[:, :KB]
    lower, inverse = factor(corner)

    left_x, top_x = [], []
    for k in range(KB):
        left, top = lefts[k].reshape(rows * size, size), tops[k]
        for m in range(k):
            left = left - lax.dot_general(left_x[m], lower[k, m], (((1,), (1,)), ((), ())), precision=high)
            top = top - jnp.dot(lower[k, m], top_x[m], precision=high)
        left_x.append(lax.dot_general(left, inverse[k], (((1,), (1,)), ((), ())), precision=high))
        top_x.append(jnp.dot(inverse[k], top, precision=high))
    left_all = jnp.concatenate(left_x, axis=1)
    top_all = jnp.concatenate(top_x, axis=0)
    front = front - jnp.dot(left_all, top_all, precision=high).reshape(rows, size, cols * size)

    column = jnp.zeros((rows, size, size), jnp.float32)
    for k in range(KB):
        column = jnp.where(pcol_id == k, left_x[k].reshape(rows, size, size), column)
        for m in range(k, KB):
            at = (row_ids == m) & (pcol_id == k)
            column = jnp.where(at[:, None, None], lower[m, k][None], column)
        above = (row_ids < k) & (pcol_id == k)
        column = jnp.where(above[:, None, None], 0.0, column)
    front = jnp.where((row_ids < KB)[:, None, None], 0.0, front)
    first = jnp.where(pcol_id < KB, column, front[:, :, :size])
    front = jnp.concatenate([first, front[:, :, size:]], axis=2)
    return front.reshape(rows, 1, size, cols, 1, size)


def solution(mesh):
    spec = P(None, "prow", None, None, "pcol", None)
    return jax.shard_map(
        per_device, mesh=mesh, in_specs=(spec, spec, P()), out_specs=spec, check_vma=False
    )
```
